32 devices in a mesh: groups: 2 (over y), batch: 4 (over z), mp: 4 (over x, core).
Axes of the slice: x: 2, y: 2, z: 4, core: 2. Of those that a mesh axis runs over, the one named last changes fastest.
Arguments:
- codes: bfloat16 [512, 26624], P(('groups', 'batch'), 'mp'), parts along dimension 0, may hold values from -127 to 127, as said below
- token_scale: float32 [512], P(('groups', 'mp')), parts along dimension 0, may hold values from 0.005 to 0.05
- weight_codes: bfloat16 [26624, 8192], P('mp', 'batch'), may hold values from -127 to 127, as said below
- weight_scale: float32 [8192], P('batch'), may hold values from 1.8385888e-05 to 0.00018385888
- smoothing: float32 [26624], P(('mp', 'batch')), may hold values from 0.25 to 4
Outputs:
- projected: bfloat16 [512, 8192], P(('groups', 'mp'), 'batch'), parts along dimension 0
The draws below stay inside these ranges and needn't reach their ends.
There are 2 independent parts, one for each index of `groups`. The reference program is written for one: setup_inputs(seed, part) draws one part's arguments, and reference() takes and returns one part's arrays. A program takes and returns all parts, laid end to end along the dimension named above; an argument that names none is the same for every part. Nothing has to cross between parts.
Inputs may be any that keep to these rules, and one draw needn't show every extreme that they name: `codes`: whole numbers. `weight_codes`: whole numbers.
All inputs are finite; a program needn't handle non-finite values.
Results may differ from the reference program's by a relative error of at most 0.0049.
Values may be sent and summed in bfloat16 or wider, within the bound.
No kernel may reach another device: no remote copies, remote signals or barrier semaphores. Data moves between devices by JAX's collectives and lax.ppermute only.
A program may use at most 128 MiB of HBM per device.

```python
import math
import jax
import jax.numpy as jnp

D = 8192
FF = 26624
TOKENS = 256


def integer_codes(key, rows, cols):
    values = jax.random.uniform(key, (rows, cols), jnp.float32, -127.5, 128.0)
    return jnp.clip(jnp.floor(values + 0.5), -127.0, 127.0)


def draw_codes(key, part):
    key = jax.random.fold_in(key, 11)
    return integer_codes(key, TOKENS, FF).astype(jnp.bfloat16)


def draw_weight_codes(key, part):
    key = jax.random.fold_in(key, 23)
    return integer_codes(key, FF, D).astype(jnp.bfloat16)


def levels(key, shape, split, low, top_value):
    level = 1.0
    for dim, shards_of in split:
        steps = jax.random.uniform(jax.random.fold_in(jax.random.fold_in(key, 6), dim), (shards_of,), jnp.float32, low / len(split), top_value / len(split))
        level = level * jnp.repeat(jnp.exp(steps), shape[dim] // shards_of).reshape((-1,) + (1,) * (len(shape) - 1 - dim))
    return level


def setup_inputs(seed: int = 0, part: int = 0) -> dict:
    arg_keys = jax.random.split(jax.random.key(seed), 6)
    part_keys = jax.random.split(jax.random.fold_in(arg_keys[5], part), 6)
    return {
        "codes": draw_codes(jax.random.fold_in(jax.random.fold_in(arg_keys[5], part), 71), part),
        "token_scale": jnp.clip(jnp.exp(math.log(0.05) - 2.3025851 * jax.random.uniform(part_keys[1], (TOKENS,), jnp.float32) ** levels(part_keys[1], (TOKENS,), ((0, 4),), -0.2, 0.2)), 0.005, 0.05),
        "weight_codes": draw_weight_codes(jax.random.fold_in(arg_keys[5], 71), part),
        "weight_scale": jnp.clip(jnp.exp(math.log(0.00018385888) - 2.3025851 * jax.random.uniform(arg_keys[3], (D,), jnp.float32) ** levels(arg_keys[3], (D,), ((0, 4),), -0.2, 0.2)), 1.8385888324701227e-05, 0.00018385888),
        "smoothing": jnp.clip(jnp.exp(math.log(4.0) - 2.7725887 * jax.random.uniform(arg_keys[4], (FF,), jnp.float32) ** levels(arg_keys[4], (FF,), ((0, 16),), -0.2, 0.2)), 0.25, 4.0),
    }


def reference(codes, token_scale, weight_codes, weight_scale, smoothing):
    smoothed = (codes.astype(jnp.float32) * smoothing[None, :]).astype(jnp.bfloat16)
    total = jnp.dot(smoothed, weight_codes, preferred_element_type=jnp.float32)
    return (total * token_scale[:, None] * weight_scale[None, :]).astype(jnp.bfloat16)
```

```python
import jax
import jax.numpy as jnp
from jax import lax
from jax.experimental import pallas as pl
from jax.experimental.pallas import tpu as pltpu
from jax.sharding import PartitionSpec as P

LANES = 128
VMEM = 44 << 20
SMALL = 1 << 20
OUTER = [(0, 1), (1, 0), (2, 3), (3, 2)]
INNER = [(1, 2), (2, 1)]
ENDS = [(1, 0), (2, 3)]


def general(codes, token_scale, weight_codes, weight_scale, smoothing):
    factors = lax.all_gather(smoothing, "batch", axis=0, tiled=True)
    partial_value = jnp.dot(
        (
            lax.all_gather(codes, "batch", axis=0, tiled=True).astype(jnp.float32)
            * factors[None, :]
        ).astype(jnp.bfloat16),
        weight_codes,
        preferred_element_type=jnp.float32,
    )
    total = lax.psum_scatter(partial_value, "mp", scatter_dimension=0, tiled=True)
    scaled = total * token_scale[:, None] * weight_scale[None, :]
    return scaled.astype(jnp.bfloat16)


def pieces_of(cols):
    sizes, left = [512], cols - 512
    while left > 1536:
        sizes.append(1024)
        left -= 1024
    while left > 512:
        sizes.append(512)
        left -= 512
    if left > 0:
        sizes.append(left)
    out, at = [], 0
    for size in sizes:
        out.append((at, size))
        at += size
    return out


def mm_kernel(place, first, pieces, n_x, n_s, n_after, has_add, n_out, split, *refs):
    xs, refs = refs[:n_x], refs[n_x:]
    ss, refs = refs[:n_s], refs[n_s:]
    w_hbm, refs = refs[0], refs[1 + n_after :]
    add = None
    if has_add:
        add, refs = refs[0], refs[1:]
    outs, refs = refs[:n_out], refs[n_out:]
    x_v, s_v, w_v, acc, sem_x, sem_s, sem_w = refs
    copy_w = [
        pltpu.make_async_copy(
            w_hbm.at[pl.ds(first + at, size)], w_v.at[pl.ds(at, size)], sem_w.at[i]
        )
        for i, (at, size) in enumerate(pieces)
    ]
    n = ss[0].shape[1]
    z = lax.axis_index("batch")
    copy_s = [
        pltpu.make_async_copy(
            ref,
            s_v.at[:, pl.ds(pl.multiple_of(lax.rem(z + 4 - k, 4) * n, n), n)],
            sem_s.at[k],
        )
        for k, ref in enumerate(ss)
    ]
    copy_w[0].start()
    for copy in copy_s:
        copy.start()
    wait_x = place(xs, x_v, sem_x)
    for copy in copy_w[1:]:
        copy.start()
    for copy in copy_s:
        copy.wait()
    wait_x()
    for i, (at, size) in enumerate(pieces):
        part = slice(at, at + size)
        s = s_v[:, first + at : first + at + size]
        x = (x_v[:, part].astype(jnp.float32) * s).astype(jnp.bfloat16)
        copy_w[i].wait()
        y = jnp.dot(x, w_v[part, :], preferred_element_type=jnp.float32)
        if i == 0:
            acc[...] = y if add is None else y + add[...]
        elif i < len(pieces) - 1:
            acc[...] += y
        else:
            y = acc[...] + y
            at = 0
            for out, rows in zip(outs, split):
                out[...] = y[at : at + rows].astype(out.dtype)
                at += rows


def mm(place, xs, ss, w, first, cols, split, out_type, add=None, name="mm"):
    pieces = pieces_of(cols)
    width = w.shape[1]
    rows = sum(split)
    body = lambda *refs: mm_kernel(
        place, first, pieces, len(xs), len(ss), 0, add is not None, len(split), split, *refs
    )
    anywhere = pl.BlockSpec(memory_space=pl.ANY)
    vmem = pl.BlockSpec(memory_space=pltpu.VMEM)
    return pl.pallas_call(
        body,
        out_shape=[jax.ShapeDtypeStruct((r, width), out_type) for r in split],
        in_specs=[anywhere] * (len(xs) + len(ss) + 1) + ([vmem] if add is not None else []),
        out_specs=[vmem] * len(split),
        scratch_shapes=[
            pltpu.VMEM((rows, cols), jnp.bfloat16),
            pltpu.VMEM((1, sum(s.shape[1] for s in ss)), jnp.float32),
            pltpu.VMEM((cols, width), jnp.bfloat16),
            pltpu.VMEM((rows, width), jnp.float32),
            pltpu.SemaphoreType.DMA((3,)),
            pltpu.SemaphoreType.DMA((len(ss),)),
            pltpu.SemaphoreType.DMA((len(pieces),)),
        ],
        compiler_params=pltpu.CompilerParams(vmem_limit_bytes=VMEM),
        cost_estimate=pl.CostEstimate(
            flops=2 * rows * cols * width,
            bytes_accessed=2 * cols * width,
            transcendentals=0,
        ),
        name=name,
    )(*xs, *ss, w, *(() if add is None else (add,)))


def after(value, *first):
    anywhere = pl.BlockSpec(memory_space=pl.ANY)
    return pl.pallas_call(
        lambda *refs: None,
        out_shape=jax.ShapeDtypeStruct(value.shape, value.dtype),
        in_specs=[anywhere] * (1 + len(first)),
        out_specs=anywhere,
        input_output_aliases={0: 0},
        compiler_params=pltpu.CompilerParams(vmem_limit_bytes=SMALL),
        name="after",
    )(value, *first)


def line_of_four(codes, token_scale, weight_codes, weight_scale, smoothing):
    rows, depth = codes.shape
    bf16, f32 = jnp.bfloat16, jnp.float32
    cut = (depth // LANES * 34 // 52) * LANES
    spans = [(0, cut), (cut, depth - cut)]

    def send(value, pairs):
        return lax.ppermute(value, "batch", pairs)

    def parts(value):
        return [lax.slice_in_dim(value, a, a + n, axis=1) for a, n in spans]

    a1 = send(codes, OUTER)
    b1 = send(codes, INNER)
    scales = smoothing[None, :]
    scales = [scales] + [
        send(scales, [(i, (i + k) % 4) for i in range(4)]) for k in (1, 2, 3)
    ]
    e2 = send(b1, ENDS)
    b2 = [send(v, INNER) for v in parts(a1)]

    def either(inner, outer, x_v, row, sem):
        z = lax.axis_index("batch")
        is_outer = (z == 0) | (z == 3)
        here = x_v.at[pl.ds(row, rows)]

        @pl.when(is_outer)
        def _():
            pltpu.make_async_copy(outer, here, sem).start()

        @pl.when(jnp.logical_not(is_outer))
        def _():
            pltpu.make_async_copy(inner, here, sem).start()

        return pltpu.make_async_copy(inner, here, sem).wait

    def place_pair(xs, x_v, sem):
        own_ref, a1_ref = xs
        mine = lax.rem(lax.axis_index("batch") + lax.axis_index("mp"), 2) == 0
        at = jnp.where(mine, 0, rows)
        copies = [
            pltpu.make_async_copy(
                ref, x_v.at[pl.ds(pl.multiple_of(to, rows), rows)], sem.at[i]
            )
            for i, (ref, to) in enumerate(((own_ref, at), (a1_ref, rows - at)))
        ]
        for copy in copies:
            copy.start()

        def wait():
            for copy in copies:
                copy.wait()

        return wait

    def place_late(span):
        def place(xs, x_v, sem):
            b1_ref, e2_ref, b2_ref, e3_ref = xs
            flip = lax.axis_index("batch") // 2 + lax.axis_index("mp")
            at = pl.multiple_of(jnp.where(lax.rem(flip, 2) == 0, 0, rows), rows)
            cols = (slice(None), pl.ds(*span))
            wait_2 = either(b1_ref.at[cols], e2_ref.at[cols], x_v, at, sem.at[0])
            at = pl.multiple_of(rows - at, rows)
            wait_3 = either(b2_ref, e3_ref, x_v, at, sem.at[1])

            def wait():
                wait_2()
                wait_3()

            return wait

        return place

    two = [rows, rows]
    w = weight_codes
    mine, other = mm(place_pair, [codes, a1], scales, w, 0, depth, two, bf16, name="mm_early")
    b2 = [after(b2[0], *scales[1:], e2), after(b2[1], mine, e2)]
    e3 = [send(v, ENDS) for v in b2]
    (ca, na), (cb, nb) = spans
    (acc,) = mm(
        place_late(spans[0]), [b1, e2, b2[0], e3[0]], scales, w, ca, na,
        [2 * rows], f32, name="mm_late",
    )
    mine_late, other_late = mm(
        place_late(spans[1]), [b1, e2, b2[1], e3[1]], scales, w, cb, nb,
        two, bf16, add=acc, name="mm_last",
    )

    z, j = lax.axis_index("batch"), lax.axis_index("mp")

    def flip(value, by):
        return lax.ppermute(value, "mp", [(i, i ^ by) for i in range(4)])

    swapped = flip(jnp.concatenate([other, other_late]), 1).astype(f32)
    early = mine.astype(f32) + swapped[:rows]
    late = mine_late.astype(f32) + swapped[rows:]
    first_here = z // 2 == j // 2
    kept = jnp.where(first_here, early, late)
    sent = jnp.where(first_here, late, early).astype(bf16)
    total = kept + flip(sent, 2).astype(f32)
    scaled = total * token_scale[:, None] * weight_scale[None, :]
    return scaled.astype(bf16)


def solution(mesh):
    fits = mesh.shape["batch"] == 4 and mesh.shape["mp"] == 4
    per_device = line_of_four if fits else general
    in_specs = (
        P(("groups", "batch"), "mp"),
        P(("groups", "mp")),
        P("mp", "batch"),
        P("batch"),
        P(("mp", "batch")),
    )
    out_specs = P(("groups", "mp"), "batch")
    return jax.shard_map(
        per_device, mesh=mesh, in_specs=in_specs, out_specs=out_specs, check_vma=False
    )
```

```python
import jax
import jax.numpy as jnp
from jax import lax
from jax.experimental import pallas as pl
from jax.experimental.pallas import tpu as pltpu
from jax.sharding import PartitionSpec as P

LANES = 128
VMEM = 44 << 20
SMALL = 1 << 20
OUTER = [(0, 1), (1, 0), (2, 3), (3, 2)]
INNER = [(1, 2), (2, 1)]
ENDS = [(1, 0), (2, 3)]


def general(codes, token_scale, weight_codes, weight_scale, smoothing):
    factors = lax.all_gather(smoothing, "batch", axis=0, tiled=True)
    partial_value = jnp.dot(
        (
            lax.all_gather(codes, "batch", axis=0, tiled=True).astype(jnp.float32)
            * factors[None, :]
        ).astype(jnp.bfloat16),
        weight_codes,
        preferred_element_type=jnp.float32,
    )
    total = lax.psum_scatter(partial_value, "mp", scatter_dimension=0, tiled=True)
    scaled = total * token_scale[:, None] * weight_scale[None, :]
    return scaled.astype(jnp.bfloat16)


def pieces_of(cols):
    sizes, left = [512], cols - 512
    while left > 1536:
        sizes.append(1024)
        left -= 1024
    while left > 512:
        sizes.append(512)
        left -= 512
    if left > 0:
        sizes.append(left)
    out, at = [], 0
    for size in sizes:
        out.append((at, size))
        at += size
    return out


def mm_kernel(place, first, pieces, n_x, n_s, n_after, has_add, n_out, split, *refs):
    xs, refs = refs[:n_x], refs[n_x:]
    ss, refs = refs[:n_s], refs[n_s:]
    w_hbm, refs = refs[0], refs[1 + n_after :]
    add = None
    if has_add:
        add, refs = refs[0], refs[1:]
    outs, refs = refs[:n_out], refs[n_out:]
    x_v, s_v, w_v, acc, sem_x, sem_s, sem_w = refs
    copy_w = [
        pltpu.make_async_copy(
            w_hbm.at[pl.ds(first + at, size)], w_v.at[pl.ds(at, size)], sem_w.at[i]
        )
        for i, (at, size) in enumerate(pieces)
    ]
    n = ss[0].shape[1]
    z = lax.axis_index("batch")
    copy_s = [
        pltpu.make_async_copy(
            ref,
            s_v.at[:, pl.ds(pl.multiple_of(lax.rem(z + 4 - k, 4) * n, n), n)],
            sem_s.at[k],
        )
        for k, ref in enumerate(ss)
    ]
    copy_w[0].start()
    for copy in copy_s:
        copy.start()
    wait_x = place(xs, x_v, sem_x)
    for copy in copy_w[1:]:
        copy.start()
    for copy in copy_s:
        copy.wait()
    wait_x()
    for i, (at, size) in enumerate(pieces):
        part = slice(at, at + size)
        s = s_v[:, first + at : first + at + size]
        x = (x_v[:, part].astype(jnp.float32) * s).astype(jnp.bfloat16)
        copy_w[i].wait()
        y = jnp.dot(x, w_v[part, :], preferred_element_type=jnp.float32)
        if i == 0:
            acc[...] = y if add is None else y + add[...]
        elif i < len(pieces) - 1:
            acc[...] += y
        else:
            y = acc[...] + y
            at = 0
            for out, rows in zip(outs, split):
                out[...] = y[at : at + rows].astype(out.dtype)
                at += rows


def mm(place, xs, ss, w, first, cols, split, out_type, add=None, name="mm"):
    pieces = pieces_of(cols)
    width = w.shape[1]
    rows = sum(split)
    body = lambda *refs: mm_kernel(
        place, first, pieces, len(xs), len(ss), 0, add is not None, len(split), split, *refs
    )
    anywhere = pl.BlockSpec(memory_space=pl.ANY)
    vmem = pl.BlockSpec(memory_space=pltpu.VMEM)
    return pl.pallas_call(
        body,
        out_shape=[jax.ShapeDtypeStruct((r, width), out_type) for r in split],
        in_specs=[anywhere] * (len(xs) + len(ss) + 1) + ([vmem] if add is not None else []),
        out_specs=[vmem] * len(split),
        scratch_shapes=[
            pltpu.VMEM((rows, cols), jnp.bfloat16),
            pltpu.VMEM((1, sum(s.shape[1] for s in ss)), jnp.float32),
            pltpu.VMEM((cols, width), jnp.bfloat16),
            pltpu.VMEM((rows, width), jnp.float32),
            pltpu.SemaphoreType.DMA((3,)),
            pltpu.SemaphoreType.DMA((len(ss),)),
            pltpu.SemaphoreType.DMA((len(pieces),)),
        ],
        compiler_params=pltpu.CompilerParams(vmem_limit_bytes=VMEM),
        cost_estimate=pl.CostEstimate(
            flops=2 * rows * cols * width,
            bytes_accessed=2 * cols * width,
            transcendentals=0,
        ),
        name=name,
    )(*xs, *ss, w, *(() if add is None else (add,)))


def after(value, *first):
    anywhere = pl.BlockSpec(memory_space=pl.ANY)
    return pl.pallas_call(
        lambda *refs: None,
        out_shape=jax.ShapeDtypeStruct(value.shape, value.dtype),
        in_specs=[anywhere] * (1 + len(first)),
        out_specs=anywhere,
        input_output_aliases={0: 0},
        compiler_params=pltpu.CompilerParams(vmem_limit_bytes=SMALL),
        name="after",
    )(value, *first)


def line_of_four(codes, token_scale, weight_codes, weight_scale, smoothing):
    rows, depth = codes.shape
    bf16, f32 = jnp.bfloat16, jnp.float32
    cut = (depth // LANES * 26 // 52) * LANES
    spans = [(0, cut), (cut, depth - cut)]

    def send(value, pairs):
        return lax.ppermute(value, "batch", pairs)

    def parts(value, spans):
        return [lax.slice_in_dim(value, a, a + n, axis=1) for a, n in spans]

    a1 = send(codes, OUTER)
    b1 = send(codes, INNER)
    scales = smoothing[None, :]
    scales = [scales] + [
        send(scales, [(i, (i + k) % 4) for i in range(4)]) for k in (1, 2, 3)
    ]
    half = (depth // LANES * 30 // 52) * LANES
    b1 = parts(b1, [(0, half), (half, depth - half)])
    a1 = after(a1, *scales[1:])
    e2 = [send(v, ENDS) for v in b1]
    b2 = [send(v, INNER) for v in parts(a1, spans)]

    def either(inner, outer, x_v, row, span, sem):
        z = lax.axis_index("batch")
        is_outer = (z == 0) | (z == 3)
        runs, at = [], 0
        for i, ref in enumerate(inner):
            lo, hi = max(span[0], at), min(span[0] + span[1], at + ref.shape[1])
            if lo < hi:
                to = x_v.at[pl.ds(row, rows), pl.ds(lo - span[0], hi - lo)]
                runs.append((i, pl.ds(lo - at, hi - lo), to))
            at += ref.shape[1]

        def copies(refs):
            return [
                pltpu.make_async_copy(refs[i].at[:, cols], to, sem)
                for i, cols, to in runs
            ]

        @pl.when(is_outer)
        def _():
            for copy in copies(outer):
                copy.start()

        @pl.when(jnp.logical_not(is_outer))
        def _():
            for copy in copies(inner):
                copy.start()

        return [copy.wait for copy in copies(inner)]

    def place_pair(xs, x_v, sem):
        own_ref, a1_ref = xs
        mine = lax.rem(lax.axis_index("batch") + lax.axis_index("mp"), 2) == 0
        at = jnp.where(mine, 0, rows)
        copies = [
            pltpu.make_async_copy(
                ref, x_v.at[pl.ds(pl.multiple_of(to, rows), rows)], sem.at[i]
            )
            for i, (ref, to) in enumerate(((own_ref, at), (a1_ref, rows - at)))
        ]
        for copy in copies:
            copy.start()

        def wait():
            for copy in copies:
                copy.wait()

        return wait

    def place_late(span):
        def place(xs, x_v, sem):
            flip = lax.axis_index("batch") // 2 + lax.axis_index("mp")
            at = pl.multiple_of(jnp.where(lax.rem(flip, 2) == 0, 0, rows), rows)
            waits = either(xs[:2], xs[2:4], x_v, at, span, sem.at[0])
            at = pl.multiple_of(rows - at, rows)
            waits += either(xs[4:5], xs[5:], x_v, at, (0, span[1]), sem.at[1])

            def wait():
                for w in waits:
                    w()

            return wait

        return place

    two = [rows, rows]
    w = weight_codes
    mine, other = mm(place_pair, [codes, a1], scales, w, 0, depth, two, bf16, name="mm_early")
    b2 = [after(b2[0], e2[0]), after(b2[1], mine, *e2)]
    e3 = [send(v, ENDS) for v in b2]
    (ca, na), (cb, nb) = spans
    (acc,) = mm(
        place_late(spans[0]), [*b1, *e2, b2[0], e3[0]], scales, w, ca, na,
        [2 * rows], f32, name="mm_late",
    )
    mine_late, other_late = mm(
        place_late(spans[1]), [*b1, *e2, b2[1], e3[1]], scales, w, cb, nb,
        two, bf16, add=acc, name="mm_last",
    )

    z, j = lax.axis_index("batch"), lax.axis_index("mp")

    def flip(value, by):
        return lax.ppermute(value, "mp", [(i, i ^ by) for i in range(4)])

    swapped = flip(jnp.concatenate([other, other_late]), 1).astype(f32)
    early = mine.astype(f32) + swapped[:rows]
    late = mine_late.astype(f32) + swapped[rows:]
    first_here = z // 2 == j // 2
    kept = jnp.where(first_here, early, late)
    sent = jnp.where(first_here, late, early).astype(bf16)
    total = kept + flip(sent, 2).astype(f32)
    scaled = total * token_scale[:, None] * weight_scale[None, :]
    return scaled.astype(bf16)


def solution(mesh):
    fits = mesh.shape["batch"] == 4 and mesh.shape["mp"] == 4
    per_device = line_of_four if fits else general
    in_specs = (
        P(("groups", "batch"), "mp"),
        P(("groups", "mp")),
        P("mp", "batch"),
        P("batch"),
        P(("mp", "batch")),
    )
    out_specs = P(("groups", "mp"), "batch")
    return jax.shard_map(
        per_device, mesh=mesh, in_specs=in_specs, out_specs=out_specs, check_vma=False
    )
```

```python
import jax
import jax.numpy as jnp
from jax import lax
from jax.experimental import pallas as pl
from jax.experimental.pallas import tpu as pltpu
from jax.sharding import PartitionSpec as P

LANES = 128
VMEM = 36 << 20
KEEP = 36 << 20
FEW = 12 << 20
SMALL = 1 << 20
OUTER = [(0, 1), (1, 0), (2, 3), (3, 2)]
INNER = [(1, 2), (2, 1)]
ENDS = [(1, 0), (2, 3)]


def general(codes, token_scale, weight_codes, weight_scale, smoothing):
    factors = lax.all_gather(smoothing, "batch", axis=0, tiled=True)
    partial_value = jnp.dot(
        (
            lax.all_gather(codes, "batch", axis=0, tiled=True).astype(jnp.float32)
            * factors[None, :]
        ).astype(jnp.bfloat16),
        weight_codes,
        preferred_element_type=jnp.float32,
    )
    total = lax.psum_scatter(partial_value, "mp", scatter_dimension=0, tiled=True)
    scaled = total * token_scale[:, None] * weight_scale[None, :]
    return scaled.astype(jnp.bfloat16)


def pieces_of(cols):
    sizes, left = [512], cols - 512
    while left > 1536:
        sizes.append(1024)
        left -= 1024
    while left > 512:
        sizes.append(512)
        left -= 512
    if left > 0:
        sizes.append(left)
    out, at = [], 0
    for size in sizes:
        out.append((at, size))
        at += size
    return out


def mm_kernel(place, first, pieces, n_x, n_s, has_w, has_add, split, keep, *refs):
    xs, refs = refs[:n_x], refs[n_x:]
    ss, refs = refs[:n_s], refs[n_s:]
    w_in, refs = refs[0], refs[1:]
    add = None
    if has_add:
        add, refs = refs[0], refs[1:]
    outs, refs = refs[: len(split)], refs[len(split) :]
    if has_w:
        w_v = w_in
    else:
        w_v, refs = refs[0], refs[1:]
    x_v, s_v, acc, sem_x, sem_s, sem_w = refs
    copy_w = []
    if not has_w:
        copy_w = [
            pltpu.make_async_copy(
                w_in.at[pl.ds(first + at, size)], w_v.at[pl.ds(at, size)], sem_w.at[i]
            )
            for i, (at, size) in enumerate(pieces)
        ]
        copy_w[0].start()
    n = ss[0].shape[1]
    z = lax.axis_index("batch")
    copy_s = [
        pltpu.make_async_copy(
            ref,
            s_v.at[:, pl.ds(pl.multiple_of(lax.rem(z + 4 - k, 4) * n, n), n)],
            sem_s.at[k],
        )
        for k, ref in enumerate(ss)
    ]
    for copy in copy_s:
        copy.start()
    wait_x = place(xs, x_v, sem_x)
    for copy in copy_w[1:]:
        copy.start()
    for copy in copy_s:
        copy.wait()
    wait_x()
    for i, (at, size) in enumerate(pieces):
        part = slice(at, at + size)
        s = s_v[:, first + at : first + at + size]
        x = (x_v[:, part].astype(jnp.float32) * s).astype(jnp.bfloat16)
        if copy_w:
            copy_w[i].wait()
        y = jnp.dot(x, w_v[part, :], preferred_element_type=jnp.float32)
        if i == 0:
            acc[...] = y if add is None else y + add[...]
        elif i < len(pieces) - 1:
            acc[...] += y
        else:
            y = acc[...] + y
            at = 0
            for out, rows in zip(outs, split):
                out[...] = y[at : at + rows].astype(out.dtype)
                at += rows


def mm(
    place, xs, ss, w, first, cols, split, out_type, add=None, keep=False, name="mm"
):
    pieces = pieces_of(cols)
    width = w.shape[1]
    rows = sum(split)
    has_w = w.shape[0] == cols
    body = lambda *refs: mm_kernel(
        place, first, pieces, len(xs), len(ss), has_w, add is not None, split, keep, *refs
    )
    anywhere = pl.BlockSpec(memory_space=pl.ANY)
    vmem = pl.BlockSpec(memory_space=pltpu.VMEM)
    outs = [jax.ShapeDtypeStruct((r, width), out_type) for r in split]
    scratch = [
        pltpu.VMEM((rows, cols), jnp.bfloat16),
        pltpu.VMEM((1, sum(s.shape[1] for s in ss)), jnp.float32),
        pltpu.VMEM((rows, width), jnp.float32),
        pltpu.SemaphoreType.DMA((3,)),
        pltpu.SemaphoreType.DMA((len(ss),)),
        pltpu.SemaphoreType.DMA((len(pieces),)),
    ]
    if keep:
        outs.append(jax.ShapeDtypeStruct((cols, width), w.dtype))
    elif not has_w:
        scratch.insert(0, pltpu.VMEM((cols, width), w.dtype))
    return pl.pallas_call(
        body,
        out_shape=outs,
        in_specs=[anywhere] * (len(xs) + len(ss))
        + [vmem if has_w else anywhere]
        + ([vmem] if add is not None else []),
        out_specs=[vmem] * len(outs),
        scratch_shapes=scratch,
        compiler_params=pltpu.CompilerParams(
            vmem_limit_bytes=FEW if has_w else KEEP if keep else VMEM
        ),
        cost_estimate=pl.CostEstimate(
            flops=2 * rows * cols * width,
            bytes_accessed=2 * cols * width,
            transcendentals=0,
        ),
        name=name,
    )(*xs, *ss, w, *(() if add is None else (add,)))


def after(value, *first):
    anywhere = pl.BlockSpec(memory_space=pl.ANY)
    return pl.pallas_call(
        lambda *refs: None,
        out_shape=jax.ShapeDtypeStruct(value.shape, value.dtype),
        in_specs=[anywhere] * (1 + len(first)),
        out_specs=anywhere,
        input_output_aliases={0: 0},
        compiler_params=pltpu.CompilerParams(vmem_limit_bytes=SMALL),
        name="after",
    )(value, *first)


def line_of_four(codes, token_scale, weight_codes, weight_scale, smoothing):
    rows, depth = codes.shape
    bf16, f32 = jnp.bfloat16, jnp.float32
    cut = (depth // LANES * 26 // 52) * LANES
    spans = [(0, cut), (cut, depth - cut)]

    def send(value, pairs):
        return lax.ppermute(value, "batch", pairs)

    def parts(value, spans):
        return [lax.slice_in_dim(value, a, a + n, axis=1) for a, n in spans]

    a1 = send(codes, OUTER)
    b1 = send(codes, INNER)
    scales = smoothing[None, :]
    scales = [scales] + [
        send(scales, [(i, (i + k) % 4) for i in range(4)]) for k in (1, 2, 3)
    ]
    half = (depth // LANES * 30 // 52) * LANES
    b1 = parts(b1, [(0, half), (half, depth - half)])
    a1 = after(a1, *scales[1:])
    e2 = [send(v, ENDS) for v in b1]
    b2 = [send(v, INNER) for v in parts(a1, spans)]

    def either(inner, outer, x_v, row, span, sem):
        z = lax.axis_index("batch")
        is_outer = (z == 0) | (z == 3)
        runs, at = [], 0
        for i, ref in enumerate(inner):
            lo, hi = max(span[0], at), min(span[0] + span[1], at + ref.shape[1])
            if lo < hi:
                to = x_v.at[pl.ds(row, rows), pl.ds(lo - span[0], hi - lo)]
                runs.append((i, pl.ds(lo - at, hi - lo), to))
            at += ref.shape[1]

        def copies(refs):
            return [
                pltpu.make_async_copy(refs[i].at[:, cols], to, sem)
                for i, cols, to in runs
            ]

        @pl.when(is_outer)
        def _():
            for copy in copies(outer):
                copy.start()

        @pl.when(jnp.logical_not(is_outer))
        def _():
            for copy in copies(inner):
                copy.start()

        return [copy.wait for copy in copies(inner)]

    def place_pair(span):
        def place(xs, x_v, sem):
            own_ref, a1_ref = xs
            mine = lax.rem(lax.axis_index("batch") + lax.axis_index("mp"), 2) == 0
            at = jnp.where(mine, 0, rows)
            copies = [
                pltpu.make_async_copy(
                    ref.at[:, pl.ds(*span)],
                    x_v.at[pl.ds(pl.multiple_of(to, rows), rows)],
                    sem.at[i],
                )
                for i, (ref, to) in enumerate(((own_ref, at), (a1_ref, rows - at)))
            ]
            for copy in copies:
                copy.start()

            def wait():
                for copy in copies:
                    copy.wait()

            return wait

        return place

    def place_late(span):
        def place(xs, x_v, sem):
            flip = lax.axis_index("batch") // 2 + lax.axis_index("mp")
            at = pl.multiple_of(jnp.where(lax.rem(flip, 2) == 0, 0, rows), rows)
            waits = either(xs[:2], xs[2:4], x_v, at, span, sem.at[0])
            at = pl.multiple_of(rows - at, rows)
            waits += either(xs[4:5], xs[5:], x_v, at, (0, span[1]), sem.at[1])

            def wait():
                for w in waits:
                    w()

            return wait

        return place

    two = [rows, rows]
    w = weight_codes
    (ca, na), (cb, nb) = spans
    (acc,) = mm(
        place_pair(spans[0]), [codes, a1], scales, w, ca, na, [2 * rows], f32,
        name="mm_early",
    )
    mine, other, w_rest = mm(
        place_pair(spans[1]), [codes, a1], scales, w, cb, nb, two, bf16, add=acc, keep=True,
        name="mm_early_rest",
    )
    b2 = [after(b2[0], e2[0], acc), after(b2[1], mine, *e2)]
    e3 = [send(v, ENDS) for v in b2]
    (acc,) = mm(
        place_late(spans[0]), [*b1, *e2, b2[0], e3[0]], scales, w, ca, na,
        [2 * rows], f32, name="mm_late",
    )
    mine_late, other_late = mm(
        place_late(spans[1]), [*b1, *e2, b2[1], e3[1]], scales, w_rest, cb, nb,
        two, bf16, add=acc, name="mm_last",
    )

    z, j = lax.axis_index("batch"), lax.axis_index("mp")

    def flip(value, by):
        return lax.ppermute(value, "mp", [(i, i ^ by) for i in range(4)])

    swapped = flip(jnp.concatenate([other, other_late]), 1).astype(f32)
    early = mine.astype(f32) + swapped[:rows]
    late = mine_late.astype(f32) + swapped[rows:]
    first_here = z // 2 == j // 2
    kept = jnp.where(first_here, early, late)
    sent = jnp.where(first_here, late, early).astype(bf16)
    total = kept + flip(sent, 2).astype(f32)
    scaled = total * token_scale[:, None] * weight_scale[None, :]
    return scaled.astype(bf16)


def solution(mesh):
    fits = mesh.shape["batch"] == 4 and mesh.shape["mp"] == 4
    per_device = line_of_four if fits else general
    in_specs = (
        P(("groups", "batch"), "mp"),
        P(("groups", "mp")),
        P("mp", "batch"),
        P("batch"),
        P(("mp", "batch")),
    )
    out_specs = P(("groups", "mp"), "batch")
    return jax.shard_map(
        per_device, mesh=mesh, in_specs=in_specs, out_specs=out_specs, check_vma=False
    )
```

```python
import jax
import jax.numpy as jnp
from jax import lax
from jax.experimental import pallas as pl
from jax.experimental.pallas import tpu as pltpu
from jax.sharding import PartitionSpec as P

LANES = 128
VMEM = 36 << 20
KEEP = 36 << 20
FEW = 12 << 20
SMALL = 1 << 20
OUTER = [(0, 1), (1, 0), (2, 3), (3, 2)]
INNER = [(1, 2), (2, 1)]
ENDS = [(1, 0), (2, 3)]


def general(codes, token_scale, weight_codes, weight_scale, smoothing):
    factors = lax.all_gather(smoothing, "batch", axis=0, tiled=True)
    partial_value = jnp.dot(
        (
            lax.all_gather(codes, "batch", axis=0, tiled=True).astype(jnp.float32)
            * factors[None, :]
        ).astype(jnp.bfloat16),
        weight_codes,
        preferred_element_type=jnp.float32,
    )
    total = lax.psum_scatter(partial_value, "mp", scatter_dimension=0, tiled=True)
    scaled = total * token_scale[:, None] * weight_scale[None, :]
    return scaled.astype(jnp.bfloat16)


def pieces_of(cols):
    sizes, left = [512], cols - 512
    while left > 1536:
        sizes.append(1024)
        left -= 1024
    while left > 512:
        sizes.append(512)
        left -= 512
    if left > 0:
        sizes.append(left)
    out, at = [], 0
    for size in sizes:
        out.append((at, size))
        at += size
    return out


def mm_kernel(place, first, pieces, n_x, n_s, has_w, has_add, split, keep, *refs):
    xs, refs = refs[:n_x], refs[n_x:]
    ss, refs = refs[:n_s], refs[n_s:]
    w_in, refs = refs[0], refs[1:]
    add = None
    if has_add:
        add, refs = refs[0], refs[1:]
    outs, refs = refs[: len(split)], refs[len(split) :]
    if has_w:
        w_v = w_in
    else:
        w_v, refs = refs[0], refs[1:]
    x_v, s_v, acc, sem_x, sem_s, sem_w = refs
    copy_w = []
    if not has_w:
        copy_w = [
            pltpu.make_async_copy(
                w_in.at[pl.ds(first + at, size)], w_v.at[pl.ds(at, size)], sem_w.at[i]
            )
            for i, (at, size) in enumerate(pieces)
        ]
        copy_w[0].start()
    n = ss[0].shape[1]
    z = lax.axis_index("batch")
    copy_s = [
        pltpu.make_async_copy(
            ref,
            s_v.at[:, pl.ds(pl.multiple_of(lax.rem(z + 4 - k, 4) * n, n), n)],
            sem_s.at[k],
        )
        for k, ref in enumerate(ss)
    ]
    for copy in copy_s:
        copy.start()
    wait_x = place(xs, x_v, sem_x)
    for copy in copy_w[1:]:
        copy.start()
    for copy in copy_s:
        copy.wait()
    wait_x()
    for i, (at, size) in enumerate(pieces):
        part = slice(at, at + size)
        s = s_v[:, first + at : first + at + size]
        x = (x_v[:, part].astype(jnp.float32) * s).astype(jnp.bfloat16)
        if copy_w:
            copy_w[i].wait()
        y = jnp.dot(x, w_v[part, :], preferred_element_type=jnp.float32)
        if i == 0:
            acc[...] = y if add is None else y + add[...]
        elif i < len(pieces) - 1:
            acc[...] += y
        else:
            y = acc[...] + y
            at = 0
            for out, rows in zip(outs, split):
                out[...] = y[at : at + rows].astype(out.dtype)
                at += rows


def mm(
    place, xs, ss, w, first, cols, split, out_type, add=None, keep=False, name="mm"
):
    pieces = pieces_of(cols)
    width = w.shape[1]
    rows = sum(split)
    has_w = w.shape[0] == cols
    body = lambda *refs: mm_kernel(
        place, first, pieces, len(xs), len(ss), has_w, add is not None, split, keep, *refs
    )
    anywhere = pl.BlockSpec(memory_space=pl.ANY)
    vmem = pl.BlockSpec(memory_space=pltpu.VMEM)
    outs = [jax.ShapeDtypeStruct((r, width), out_type) for r in split]
    scratch = [
        pltpu.VMEM((rows, cols), jnp.bfloat16),
        pltpu.VMEM((1, sum(s.shape[1] for s in ss)), jnp.float32),
        pltpu.VMEM((rows, width), jnp.float32),
        pltpu.SemaphoreType.DMA((3,)),
        pltpu.SemaphoreType.DMA((len(ss),)),
        pltpu.SemaphoreType.DMA((len(pieces),)),
    ]
    if keep:
        outs.append(jax.ShapeDtypeStruct((cols, width), w.dtype))
    elif not has_w:
        scratch.insert(0, pltpu.VMEM((cols, width), w.dtype))
    return pl.pallas_call(
        body,
        out_shape=outs,
        in_specs=[anywhere] * (len(xs) + len(ss))
        + [vmem if has_w else anywhere]
        + ([vmem] if add is not None else []),
        out_specs=[vmem] * len(outs),
        scratch_shapes=scratch,
        compiler_params=pltpu.CompilerParams(
            vmem_limit_bytes=FEW if has_w else KEEP if keep else VMEM
        ),
        cost_estimate=pl.CostEstimate(
            flops=2 * rows * cols * width,
            bytes_accessed=2 * cols * width,
            transcendentals=0,
        ),
        name=name,
    )(*xs, *ss, w, *(() if add is None else (add,)))


def after(value, *first):
    anywhere = pl.BlockSpec(memory_space=pl.ANY)
    return pl.pallas_call(
        lambda *refs: None,
        out_shape=jax.ShapeDtypeStruct(value.shape, value.dtype),
        in_specs=[anywhere] * (1 + len(first)),
        out_specs=anywhere,
        input_output_aliases={0: 0},
        compiler_params=pltpu.CompilerParams(vmem_limit_bytes=SMALL),
        name="after",
    )(value, *first)


def line_of_four(codes, token_scale, weight_codes, weight_scale, smoothing):
    rows, depth = codes.shape
    bf16, f32 = jnp.bfloat16, jnp.float32
    cut = (depth // LANES * 26 // 52) * LANES
    spans = [(0, cut), (cut, depth - cut)]

    def send(value, pairs):
        return lax.ppermute(value, "batch", pairs)

    def parts(value, spans):
        return [lax.slice_in_dim(value, a, a + n, axis=1) for a, n in spans]

    a1 = send(codes, OUTER)
    b1 = send(codes, INNER)
    scales = smoothing[None, :]
    scales = [scales] + [
        send(scales, [(i, (i + k) % 4) for i in range(4)]) for k in (1, 2, 3)
    ]
    half = (depth // LANES * 30 // 52) * LANES
    b1 = parts(b1, [(0, half), (half, depth - half)])
    a1 = after(a1, *scales[1:])
    e2 = [send(v, ENDS) for v in b1]
    b2 = [send(v, INNER) for v in parts(a1, spans)]

    def either(inner, outer, x_v, row, span, sem):
        z = lax.axis_index("batch")
        is_outer = (z == 0) | (z == 3)
        runs, at = [], 0
        for i, ref in enumerate(inner):
            lo, hi = max(span[0], at), min(span[0] + span[1], at + ref.shape[1])
            if lo < hi:
                to = x_v.at[pl.ds(row, rows), pl.ds(lo - span[0], hi - lo)]
                runs.append((i, pl.ds(lo - at, hi - lo), to))
            at += ref.shape[1]

        def copies(refs):
            return [
                pltpu.make_async_copy(refs[i].at[:, cols], to, sem)
                for i, cols, to in runs
            ]

        @pl.when(is_outer)
        def _():
            for copy in copies(outer):
                copy.start()

        @pl.when(jnp.logical_not(is_outer))
        def _():
            for copy in copies(inner):
                copy.start()

        return [copy.wait for copy in copies(inner)]

    def place_pair(span):
        def place(xs, x_v, sem):
            own_ref, a1_ref = xs
            mine = lax.rem(lax.axis_index("batch") + lax.axis_index("mp"), 2) == 0
            at = jnp.where(mine, 0, rows)
            copies = [
                pltpu.make_async_copy(
                    ref.at[:, pl.ds(*span)],
                    x_v.at[pl.ds(pl.multiple_of(to, rows), rows)],
                    sem.at[i],
                )
                for i, (ref, to) in enumerate(((own_ref, at), (a1_ref, rows - at)))
            ]
            for copy in copies:
                copy.start()

            def wait():
                for copy in copies:
                    copy.wait()

            return wait

        return place

    def place_late(span):
        def place(xs, x_v, sem):
            flip = lax.axis_index("batch") // 2 + lax.axis_index("mp")
            at = pl.multiple_of(jnp.where(lax.rem(flip, 2) == 0, 0, rows), rows)
            waits = either(xs[:2], xs[2:4], x_v, at, span, sem.at[0])
            at = pl.multiple_of(rows - at, rows)
            waits += either(xs[4:5], xs[5:], x_v, at, (0, span[1]), sem.at[1])

            def wait():
                for w in waits:
                    w()

            return wait

        return place

    two = [rows, rows]
    w = weight_codes
    (ca, na), (cb, nb) = spans
    (acc,) = mm(
        place_pair(spans[0]), [codes, a1], scales, w, ca, na, [2 * rows], f32,
        name="mm_early",
    )
    mine, other, w_rest = mm(
        place_pair(spans[1]), [codes, a1], scales, w, cb, nb, two, bf16, add=acc, keep=True,
        name="mm_early_rest",
    )
    b2 = [after(b2[0], e2[0], acc), after(b2[1], mine, *e2)]
    e3 = [send(v, ENDS) for v in b2]
    swapped = lax.ppermute(other, "mp", [(i, i ^ 1) for i in range(4)])
    e3[0] = after(e3[0], swapped)
    (acc,) = mm(
        place_late(spans[0]), [*b1, *e2, b2[0], e3[0]], scales, w, ca, na,
        [2 * rows], f32, name="mm_late",
    )
    mine_late, other_late = mm(
        place_late(spans[1]), [*b1, *e2, b2[1], e3[1]], scales, w_rest, cb, nb,
        two, bf16, add=acc, name="mm_last",
    )

    z, j = lax.axis_index("batch"), lax.axis_index("mp")

    def flip(value, by):
        return lax.ppermute(value, "mp", [(i, i ^ by) for i in range(4)])

    early = mine.astype(f32) + swapped.astype(f32)
    late = mine_late.astype(f32) + flip(other_late, 1).astype(f32)
    first_here = z // 2 == j // 2
    kept = jnp.where(first_here, early, late)
    sent = jnp.where(first_here, late, early).astype(bf16)
    total = kept + flip(sent, 2).astype(f32)
    scaled = total * token_scale[:, None] * weight_scale[None, :]
    return scaled.astype(bf16)


def solution(mesh):
    fits = mesh.shape["batch"] == 4 and mesh.shape["mp"] == 4
    per_device = line_of_four if fits else general
    in_specs = (
        P(("groups", "batch"), "mp"),
        P(("groups", "mp")),
        P("mp", "batch"),
        P("batch"),
        P(("mp", "batch")),
    )
    out_specs = P(("groups", "mp"), "batch")
    return jax.shard_map(
        per_device, mesh=mesh, in_specs=in_specs, out_specs=out_specs, check_vma=False
    )
```

```python
import jax
import jax.numpy as jnp
from jax import lax
from jax.experimental import pallas as pl
from jax.experimental.pallas import tpu as pltpu
from jax.sharding import PartitionSpec as P

LANES = 128
VMEM = 36 << 20
KEEP = 36 << 20
FEW = 12 << 20
SMALL = 1 << 20
OUTER = [(0, 1), (1, 0), (2, 3), (3, 2)]
INNER = [(1, 2), (2, 1)]
ENDS = [(1, 0), (2, 3)]


def general(codes, token_scale, weight_codes, weight_scale, smoothing):
    factors = lax.all_gather(smoothing, "batch", axis=0, tiled=True)
    partial_value = jnp.dot(
        (
            lax.all_gather(codes, "batch", axis=0, tiled=True).astype(jnp.float32)
            * factors[None, :]
        ).astype(jnp.bfloat16),
        weight_codes,
        preferred_element_type=jnp.float32,
    )
    total = lax.psum_scatter(partial_value, "mp", scatter_dimension=0, tiled=True)
    scaled = total * token_scale[:, None] * weight_scale[None, :]
    return scaled.astype(jnp.bfloat16)


def pieces_of(cols):
    sizes, left = [512], cols - 512
    while left > 1536:
        sizes.append(1024)
        left -= 1024
    while left > 512:
        sizes.append(512)
        left -= 512
    if left > 0:
        sizes.append(left)
    out, at = [], 0
    for size in sizes:
        out.append((at, size))
        at += size
    return out


def mm_kernel(place, first, pieces, n_x, n_s, has_w, has_add, split, keep, *refs):
    xs, refs = refs[:n_x], refs[n_x:]
    ss, refs = refs[:n_s], refs[n_s:]
    w_in, refs = refs[0], refs[1:]
    add = None
    if has_add:
        add, refs = refs[0], refs[1:]
    outs, refs = refs[: len(split)], refs[len(split) :]
    if has_w:
        w_v = w_in
    else:
        w_v, refs = refs[0], refs[1:]
    x_v, s_v, acc, sem_x, sem_s, sem_w = refs
    copy_w = []
    if not has_w:
        copy_w = [
            pltpu.make_async_copy(
                w_in.at[pl.ds(first + at, size)], w_v.at[pl.ds(at, size)], sem_w.at[i]
            )
            for i, (at, size) in enumerate(pieces)
        ]
        copy_w[0].start()
    n = ss[0].shape[1]
    z = lax.axis_index("batch")
    copy_s = [
        pltpu.make_async_copy(
            ref,
            s_v.at[:, pl.ds(pl.multiple_of(lax.rem(z + 4 - k, 4) * n, n), n)],
            sem_s.at[k],
        )
        for k, ref in enumerate(ss)
    ]
    for copy in copy_s:
        copy.start()
    wait_x = place(xs, x_v, sem_x)
    for copy in copy_w[1:]:
        copy.start()
    for copy in copy_s:
        copy.wait()
    wait_x()
    if has_w:
        s = s_v[:, first : first + x_v.shape[1]]
        x_v[...] = (x_v[...].astype(jnp.float32) * s).astype(jnp.bfloat16)
        step = w_v.shape[1] // 4
        for c in range(0, w_v.shape[1], step):
            part = slice(c, c + step)
            y = jnp.dot(x_v[...], w_v[:, part], preferred_element_type=jnp.float32)
            if add is not None:
                y += add[:, part]
            at = 0
            for out, rows in zip(outs, split):
                out[:, part] = y[at : at + rows].astype(out.dtype)
                at += rows
        return
    for i, (at, size) in enumerate(pieces):
        part = slice(at, at + size)
        s = s_v[:, first + at : first + at + size]
        x = (x_v[:, part].astype(jnp.float32) * s).astype(jnp.bfloat16)
        if copy_w:
            copy_w[i].wait()
        y = jnp.dot(x, w_v[part, :], preferred_element_type=jnp.float32)
        if i == 0:
            acc[...] = y if add is None else y + add[...]
        elif i < len(pieces) - 1:
            acc[...] += y
        else:
            y = acc[...] + y
            at = 0
            for out, rows in zip(outs, split):
                out[...] = y[at : at + rows].astype(out.dtype)
                at += rows


def mm(
    place, xs, ss, w, first, cols, split, out_type, add=None, keep=False, name="mm"
):
    pieces = pieces_of(cols)
    width = w.shape[1]
    rows = sum(split)
    has_w = w.shape[0] == cols
    body = lambda *refs: mm_kernel(
        place, first, pieces, len(xs), len(ss), has_w, add is not None, split, keep, *refs
    )
    anywhere = pl.BlockSpec(memory_space=pl.ANY)
    vmem = pl.BlockSpec(memory_space=pltpu.VMEM)
    outs = [jax.ShapeDtypeStruct((r, width), out_type) for r in split]
    scratch = [
        pltpu.VMEM((rows, cols), jnp.bfloat16),
        pltpu.VMEM((1, sum(s.shape[1] for s in ss)), jnp.float32),
        pltpu.VMEM((rows, width), jnp.float32),
        pltpu.SemaphoreType.DMA((3,)),
        pltpu.SemaphoreType.DMA((len(ss),)),
        pltpu.SemaphoreType.DMA((len(pieces),)),
    ]
    if keep:
        outs.append(jax.ShapeDtypeStruct((cols, width), w.dtype))
    elif not has_w:
        scratch.insert(0, pltpu.VMEM((cols, width), w.dtype))
    return pl.pallas_call(
        body,
        out_shape=outs,
        in_specs=[anywhere] * (len(xs) + len(ss))
        + [vmem if has_w else anywhere]
        + ([vmem] if add is not None else []),
        out_specs=[vmem] * len(outs),
        scratch_shapes=scratch,
        compiler_params=pltpu.CompilerParams(
            vmem_limit_bytes=FEW if has_w else KEEP if keep else VMEM
        ),
        cost_estimate=pl.CostEstimate(
            flops=2 * rows * cols * width,
            bytes_accessed=2 * cols * width,
            transcendentals=0,
        ),
        name=name,
    )(*xs, *ss, w, *(() if add is None else (add,)))


def after(value, *first):
    anywhere = pl.BlockSpec(memory_space=pl.ANY)
    return pl.pallas_call(
        lambda *refs: None,
        out_shape=jax.ShapeDtypeStruct(value.shape, value.dtype),
        in_specs=[anywhere] * (1 + len(first)),
        out_specs=anywhere,
        input_output_aliases={0: 0},
        compiler_params=pltpu.CompilerParams(vmem_limit_bytes=SMALL),
        name="after",
    )(value, *first)


def line_of_four(codes, token_scale, weight_codes, weight_scale, smoothing):
    rows, depth = codes.shape
    bf16, f32 = jnp.bfloat16, jnp.float32
    cut = (depth // LANES * 26 // 52) * LANES
    spans = [(0, cut), (cut, depth - cut)]

    def send(value, pairs):
        return lax.ppermute(value, "batch", pairs)

    def parts(value, spans):
        return [lax.slice_in_dim(value, a, a + n, axis=1) for a, n in spans]

    a1 = send(codes, OUTER)
    b1 = send(codes, INNER)
    scales = smoothing[None, :]
    scales = [scales] + [
        send(scales, [(i, (i + k) % 4) for i in range(4)]) for k in (1, 2, 3)
    ]
    half = (depth // LANES * 30 // 52) * LANES
    b1 = parts(b1, [(0, half), (half, depth - half)])
    a1 = after(a1, *scales[1:])
    e2 = [send(v, ENDS) for v in b1]
    b2 = [send(v, INNER) for v in parts(a1, spans)]

    def either(inner, outer, x_v, row, span, sem):
        z = lax.axis_index("batch")
        is_outer = (z == 0) | (z == 3)
        runs, at = [], 0
        for i, ref in enumerate(inner):
            lo, hi = max(span[0], at), min(span[0] + span[1], at + ref.shape[1])
            if lo < hi:
                to = x_v.at[pl.ds(row, rows), pl.ds(lo - span[0], hi - lo)]
                runs.append((i, pl.ds(lo - at, hi - lo), to))
            at += ref.shape[1]

        def copies(refs):
            return [
                pltpu.make_async_copy(refs[i].at[:, cols], to, sem)
                for i, cols, to in runs
            ]

        @pl.when(is_outer)
        def _():
            for copy in copies(outer):
                copy.start()

        @pl.when(jnp.logical_not(is_outer))
        def _():
            for copy in copies(inner):
                copy.start()

        return [copy.wait for copy in copies(inner)]

    def place_pair(span):
        def place(xs, x_v, sem):
            own_ref, a1_ref = xs
            mine = lax.rem(lax.axis_index("batch") + lax.axis_index("mp"), 2) == 0
            at = jnp.where(mine, 0, rows)
            copies = [
                pltpu.make_async_copy(
                    ref.at[:, pl.ds(*span)],
                    x_v.at[pl.ds(pl.multiple_of(to, rows), rows)],
                    sem.at[i],
                )
                for i, (ref, to) in enumerate(((own_ref, at), (a1_ref, rows - at)))
            ]
            for copy in copies:
                copy.start()

            def wait():
                for copy in copies:
                    copy.wait()

            return wait

        return place

    def place_late(span):
        def place(xs, x_v, sem):
            flip = lax.axis_index("batch") // 2 + lax.axis_index("mp")
            at = pl.multiple_of(jnp.where(lax.rem(flip, 2) == 0, 0, rows), rows)
            waits = either(xs[:2], xs[2:4], x_v, at, span, sem.at[0])
            at = pl.multiple_of(rows - at, rows)
            waits += either(xs[4:5], xs[5:], x_v, at, (0, span[1]), sem.at[1])

            def wait():
                for w in waits:
                    w()

            return wait

        return place

    two = [rows, rows]
    w = weight_codes
    (ca, na), (cb, nb) = spans
    (acc,) = mm(
        place_pair(spans[0]), [codes, a1], scales, w, ca, na, [2 * rows], f32,
        name="mm_early",
    )
    mine, other, w_rest = mm(
        place_pair(spans[1]), [codes, a1], scales, w, cb, nb, two, bf16, add=acc, keep=True,
        name="mm_early_rest",
    )
    b2 = [after(b2[0], e2[0], acc), after(b2[1], mine, *e2)]
    e3 = [send(v, ENDS) for v in b2]
    swapped = lax.ppermute(other, "mp", [(i, i ^ 1) for i in range(4)])
    e3[0] = after(e3[0], swapped)
    (acc,) = mm(
        place_late(spans[0]), [*b1, *e2, b2[0], e3[0]], scales, w, ca, na,
        [2 * rows], f32, name="mm_late",
    )
    mine_late, other_late = mm(
        place_late(spans[1]), [*b1, *e2, b2[1], e3[1]], scales, w_rest, cb, nb,
        two, bf16, add=acc, name="mm_last",
    )

    z, j = lax.axis_index("batch"), lax.axis_index("mp")

    def flip(value, by):
        return lax.ppermute(value, "mp", [(i, i ^ by) for i in range(4)])

    early = mine.astype(f32) + swapped.astype(f32)
    late = mine_late.astype(f32) + flip(other_late, 1).astype(f32)
    first_here = z // 2 == j // 2
    kept = jnp.where(first_here, early, late)
    sent = jnp.where(first_here, late, early).astype(bf16)
    kept = lax.optimization_barrier(kept)
    total = kept + flip(sent, 2).astype(f32)
    scaled = total * token_scale[:, None] * weight_scale[None, :]
    return scaled.astype(bf16)


def solution(mesh):
    fits = mesh.shape["batch"] == 4 and mesh.shape["mp"] == 4
    per_device = line_of_four if fits else general
    in_specs = (
        P(("groups", "batch"), "mp"),
        P(("groups", "mp")),
        P("mp", "batch"),
        P("batch"),
        P(("mp", "batch")),
    )
    out_specs = P(("groups", "mp"), "batch")
    return jax.shard_map(
        per_device, mesh=mesh, in_specs=in_specs, out_specs=out_specs, check_vma=False
    )
```
